32 devices in a mesh: cells: 8 (over y, x, core), energy: 4 (over z).
Axes of the slice: x: 2, y: 2, z: 4, core: 2. Of those that a mesh axis runs over, the one named last changes fastest.
Arguments:
- distribution: bfloat16 [2048, 1024], P('cells', 'energy'), may hold values from -6 to 6
- operators: bfloat16 [4, 1024, 1024], P(None, 'energy', 'cells'), may hold values from -0.1875 to 0.1875
- sections: bfloat16 [4096, 1024], P('cells', 'energy'), may hold values from -0.1875 to 0.1875
- populations: float32 [2048, 256], P(('cells', 'energy')), may hold values from 0.1 to 1
- cell_owner: int32 [2048, 1], P(('cells', 'energy')), may hold values from 0 to 7; in each aligned block of 64 rows (0 to 63, 64 to 127, ...) at most 16 rows name the same one
- partner_of: int32 [256, 1], replicated, may hold values from 0 to 3
- source: int32 [4096], replicated, may hold values from 0 to 255
- level_hop: int32 [4096], replicated, may hold values from 1 to 255
- radiative: float32 [4096], replicated, may hold values from 0.05 to 2
Outputs:
- spectrum_out: float32 [2048, 1024], P('cells', 'energy')
- levels_out: float32 [2048, 256], P(('cells', 'energy'))
The draws below stay inside these ranges and needn't reach their ends.
Inputs may be any that keep to these rules, and one draw needn't show every extreme that they name: `cell_owner`: in each aligned block of 64 rows (the rows of one device) no zone occurs more than 16 times, and some block reaches it; every zone has some cell. `partner_of`: every partner has at least one level.
All inputs are finite; a program needn't handle non-finite values.
Results may differ from the reference program's by a relative error of at most 0.0028.
Values may be sent and summed in bfloat16 or wider, within the bound.
No kernel may reach another device: no remote copies, remote signals or barrier semaphores. Data moves between devices by JAX's collectives and lax.ppermute only.
A program may use at most 64 MiB of HBM per device.

```python
import math
import jax
import jax.numpy as jnp
import numpy as np
from jax import lax

E = 1024
P_SIZE = 4
R = 4096
L = 256
CB = 256
ITERS = 2
SUB = 2
NC = 2048
CAP = 16
N_CELLS = 8
N_ENERGY = 4


def set_ends(drawn, key, smallest, top_value):
    place = [jax.random.randint(jax.random.fold_in(key, axis), (), 0, length) for axis, length in enumerate(drawn.shape)]
    longest = drawn.shape.index(max(drawn.shape))
    next_to = place[:longest] + [(place[longest] + 1) % drawn.shape[longest]] + place[longest + 1:]
    return drawn.at[tuple(place)].set(smallest).at[tuple(next_to)].set(top_value)


def block_levels(own_key, extent, split, low, top_value):
    def one(position, shards_of):
        draws = jax.random.uniform(jax.random.fold_in(jax.random.fold_in(own_key, 6), position), (shards_of,), jnp.float32, low / len(split), top_value / len(split))
        return jnp.repeat(jnp.exp(draws), extent[position] // shards_of).reshape((-1,) + (1,) * (len(extent) - position - 1))

    level = one(*split[0])
    for cut in split[1:]:
        level = level * one(*cut)
    return level


def picks_of(own_key, rows, number_of, top, lift):
    ranking = jax.random.permutation(jax.random.fold_in(own_key, 1), number_of)
    favour = ranking
    for power in range(3):
        favour = favour * favour // number_of
    favour = favour * lift // number_of
    tickets = jax.random.randint(jax.random.fold_in(own_key, 2), (rows, number_of), 0, 4096) + favour
    holders = jax.random.permutation(jax.random.fold_in(own_key, 3), rows)[jnp.arange(number_of) % rows]
    tickets = jnp.where(jnp.arange(rows)[:, None] == holders[None, :], 1 << 14, tickets)
    score = tickets * number_of + jnp.arange(number_of)
    return lax.top_k(score.astype(jnp.int32), top)[1].astype(jnp.int32)


def shared_out(own_key, own, number, rows, amount, top, reach, skew):
    order = jax.random.permutation(own_key, amount)
    packed, usual = shares(amount, rows * top, reach, skew, True), shares(amount, rows * top, reach, skew, False)
    places = jnp.arange(amount)

    def named(sizes, rotation):
        used = int((sizes > 0).sum())
        fixed = max(1, used // 4)
        shifted = fixed + (places - fixed + rotation * (used - fixed)) % max(1, amount - fixed)
        return jnp.zeros((amount,), jnp.int32).at[order[jnp.where(places < fixed, places, shifted)]].set(jnp.asarray(sizes, jnp.int32))

    sizes = jnp.where(number % 4 == 0, named(packed, number // 4), named(usual, number - number // 4 - 1))
    mixed = jax.random.permutation(jax.random.fold_in(own, 3), amount)
    source_of, taker = mixed[0:amount // 2 * 2:2], mixed[1:amount // 2 * 2:2]
    room = jnp.minimum(sizes[source_of] - 1, reach - sizes[taker]) // 2
    room = jnp.where((source_of == order[0]) | (taker == order[0]) | (sizes[taker] == 0), 0, jnp.maximum(room, 0))
    shifted = jax.random.randint(jax.random.fold_in(own, 4), (amount // 2,), 0, 1 << 20) % (room + 1)
    sizes = sizes.at[source_of].add(-shifted).at[taker].add(shifted)
    items = jnp.searchsorted(jnp.cumsum(sizes), jnp.arange(rows * top), side="right").astype(jnp.int32)
    grid = items.reshape(top, rows).T
    grid = grid[jax.random.permutation(jax.random.fold_in(own, 1), rows)]
    rotation = jax.random.randint(jax.random.fold_in(own, 2), (rows, 1), 0, top)
    return jnp.take_along_axis(grid, (jnp.arange(top)[None, :] + rotation) % top, axis=1)


def shares(count, total, most, lean, full):
    portions = [(1 << 20) // math.isqrt(standing ** lean) + 1 for standing in range(1, count + 1)]
    largest = most if full else min(most, max(-(-total // count), total * portions[0] // sum(portions)))
    least = 1 if total - largest >= count - 1 else 0
    holding, surplus = [largest] + [least] * (count - 1), total - largest - least * (count - 1)
    while surplus > 0:
        free = [i for i in range(1, count) if holding[i] < largest] or [i for i in range(1, count) if holding[i] < most]
        pool, budget = sum([portions[i] for i in free]), surplus
        for i in free:
            more = min(most - holding[i], max(1, budget * portions[i] // pool), surplus)
            holding[i] = holding[i] + more
            surplus = surplus - more
    return np.array(holding)


def normal_values(stream_key, shape, deviation, reach, pieces=(), kind=jnp.bfloat16):
    values = deviation * jax.random.normal(stream_key, shape, jnp.float32)
    if pieces:
        values = values * block_levels(stream_key, shape, pieces, -0.22, 0.18)
    return jnp.clip(values, -reach, reach).astype(kind)


def setup_inputs(seed: int = 0) -> dict:
    keys = jax.random.split(jax.random.key(seed), 10)
    distribution = normal_values(keys[0], (NC, E), 1.0, 6.0, ((0, 8), (1, 4)))
    operators = normal_values(keys[1], (P_SIZE, E, E), E ** -0.5, 0.1875, ((1, 4), (2, 8)))
    sections = normal_values(keys[2], (R, E), E ** -0.5, 0.1875, ((0, 8), (1, 4)))
    populations = jnp.clip(jnp.exp(math.log(1.0) - 2.3025851 * jax.random.uniform(keys[3], (NC, L), jnp.float32) ** block_levels(keys[3], (NC, L), ((0, 32),), -0.2, 0.2)), 0.1, 1.0)
    cell_owner_keys = jax.random.split(jax.random.fold_in(keys[4], 1), NC // (CB // N_ENERGY))
    cell_owner_turns = jax.random.permutation(jax.random.fold_in(keys[4], 3), NC // (CB // N_ENERGY))
    cell_owner = jax.vmap(lambda own, number: shared_out(jax.random.fold_in(keys[4], 2), own, number, CB // N_ENERGY, N_CELLS, 1, CAP, 2))(cell_owner_keys, cell_owner_turns).reshape((NC, 1))
    partner_of = picks_of(keys[5], L, P_SIZE, 1, 0)
    source = set_ends(jax.random.randint(keys[6], (R,), 0, L), jax.random.fold_in(keys[6], 1), 0, L - 1).astype(jnp.int32)
    level_hop = set_ends(jax.random.randint(keys[7], (R,), 1, L), jax.random.fold_in(keys[7], 1), 1, L - 1).astype(jnp.int32)
    radiative = jnp.clip(jnp.exp(jax.random.uniform(keys[8], (R,), jnp.float32, math.log(0.05), math.log(2.0))), 0.05, 2.0)
    return {"distribution": distribution, "operators": operators, "sections": sections, "populations": populations, "cell_owner": cell_owner, "partner_of": partner_of, "source": source, "level_hop": level_hop, "radiative": radiative}


boltz_step = 0.5
level_step = 0.04
depth_scale = 2.0


def reference(distribution, operators, sections, populations, cell_owner, partner_of, source, level_hop, radiative):
    highest = lax.Precision.HIGHEST
    target = (source + level_hop) % L
    level_ids = jnp.arange(L, dtype=jnp.int32)
    source_map = (level_ids[:, None] == source[None, :]).astype(jnp.float32)
    transfer = (target[:, None] == level_ids[None, :]).astype(jnp.float32) - (source[:, None] == level_ids[None, :]).astype(jnp.float32)
    partner_map = (partner_of[:, 0][:, None] == jnp.arange(P_SIZE, dtype=jnp.int32)[None, :]).astype(jnp.float32)
    level_counts = jnp.sum(partner_map, axis=0)
    zone_of = cell_owner[:, 0]
    current = distribution.astype(jnp.float32)
    levels = populations
    block_count = NC // CB
    for sweep in range(ITERS):
        density = jnp.dot(levels, partner_map, precision=highest) / level_counts
        spectra = current.astype(jnp.bfloat16)
        summed = jnp.zeros_like(current)
        for partner in range(P_SIZE):
            product = jnp.dot(spectra, operators[partner].T, preferred_element_type=jnp.float32)
            summed = summed + density[:, partner:partner + 1] * product
        current = current + boltz_step * summed
        column = jax.ops.segment_sum(levels[:, 0], zone_of, num_segments=N_CELLS)
        escape = 1.0 / (1.0 + depth_scale * column / CB)
        cell_escape = escape[zone_of]

        def update(block):
            cell_rows, level_block, escape_rows = block
            raw_sums = lax.dot_general(cell_rows, sections, (((1,), (1,)), ((), ())), preferred_element_type=jnp.float32)
            reaction_rates = jax.nn.softplus(raw_sums) + radiative[None, :] * escape_rows[:, None]
            for substep in range(SUB):
                flux = reaction_rates * jnp.dot(level_block, source_map, precision=highest)
                level_block = level_block + level_step * jnp.dot(flux, transfer, precision=highest)
            return level_block

        levels = lax.map(update, (spectra.reshape(block_count, CB, E), levels.reshape(block_count, CB, L), cell_escape.reshape(block_count, CB))).reshape(NC, L)
    return current, levels
```

```python
import jax
import jax.numpy as jnp
from jax import lax
from jax.experimental import pallas as pl
from jax.experimental.pallas import tpu as pltpu
from jax.sharding import PartitionSpec as P

boltz_step = 0.5
level_step = 0.04
depth_scale = 2.0

BF = jnp.bfloat16
F32 = jnp.float32
NT = (((1,), (1,)), ((), ()))
TILE = 8
LANES = 128
COLUMN_ROW = 4
PARAMS = pltpu.CompilerParams(vmem_limit_bytes=40 << 20)


def swap(x, axis, mask, count):
    return lax.ppermute(x, axis, [(i, i ^ mask) for i in range(count)])


def others(x, ne):
    got = {mask: swap(x, "energy", mask, ne) for mask in range(ne - 1, 0, -1)}
    return [x] + [got[mask] for mask in range(1, ne)]


def cross(x, first):
    masks = (2, 4) if first else (4, 2)
    return lax.ppermute(x, "cells", [(i, i ^ masks[i & 1]) for i in range(8)])


def gather_cells(x):
    a = cross(x, True)
    b = cross(x, False)
    c = cross(b, True)
    own = [x, a, b, c]
    return own + [swap(v, "cells", 1, 8) for v in own]


def gathered_places(i):
    first = jnp.where((i & 1) == 0, 2, 4)
    own = [i, i ^ first, i ^ (6 - first), i ^ 6]
    sibling = [i ^ 1, i ^ 1 ^ (6 - first), i ^ 1 ^ first, i ^ 7]
    return own + sibling


def aligned(index, size):
    return pl.ds(pl.multiple_of(index * size, size), size)


def split(x):
    high = x.astype(BF)
    return high, (x - high.astype(F32)).astype(BF)


def halves(x):
    return jnp.concatenate(split(x), 0)


def dot(a, b):
    return jnp.dot(a, b, preferred_element_type=F32)


def dot_nt(a, b):
    return lax.dot_general(a, b, NT, preferred_element_type=F32)


def fold(x):
    n = x.shape[0] // 2
    return x[:n] + x[n:]


def call(kernel, shapes, ints, *args, scratch=()):
    return pl.pallas_call(
        kernel,
        out_shape=tuple(jax.ShapeDtypeStruct(s, t) for s, t in shapes),
        in_specs=[pl.BlockSpec(memory_space=pltpu.SMEM)]
        + [pl.BlockSpec(memory_space=pltpu.VMEM)] * len(args),
        out_specs=tuple(pl.BlockSpec(memory_space=pltpu.VMEM) for _ in shapes),
        scratch_shapes=list(scratch),
        compiler_params=PARAMS,
    )(ints, *args)


def zones_of(owner_ref):
    owner = owner_ref[...]
    lanes = lax.broadcasted_iota(jnp.int32, (owner.shape[0], LANES), 1)
    return jnp.where(owner == lanes, 1.0, 0.0)


def put_news(levels, partner_ref, owner_ref, out_ref):
    rows, total = levels.shape
    ids = lax.broadcasted_iota(jnp.int32, (TILE, total), 0)
    chosen = jnp.where(ids == partner_ref[...], 1.0, 0.0)
    number = jnp.maximum(jnp.sum(chosen, axis=1, keepdims=True), 1.0)
    chosen = chosen.astype(BF)
    high, low = split(levels)
    density = (dot_nt(chosen, high) + dot_nt(chosen, low)) / number
    tile = jnp.concatenate([density, jnp.zeros((TILE, LANES - rows), F32)], 1)
    column = jnp.sum(zones_of(owner_ref) * levels[:, 0:1], axis=0, keepdims=True)
    at = lax.broadcasted_iota(jnp.int32, (TILE, LANES), 0)
    tile = jnp.where(at == COLUMN_ROW, column, tile)
    for n in range(out_ref.shape[0] // TILE):
        out_ref[n * TILE : (n + 1) * TILE, :] = tile


def news_kernel(ints_ref, level_ref, partner_ref, owner_ref, out_ref):
    put_news(level_ref[...], partner_ref, owner_ref, out_ref)


def escape_of(news_ref, owner_ref, block):
    news = news_ref[...].reshape(news_ref.shape[0] // TILE, TILE, LANES)
    column = jnp.sum(news, axis=0)[COLUMN_ROW : COLUMN_ROW + 1]
    escape = 1.0 / (1.0 + depth_scale * column / block)
    return jnp.sum(zones_of(owner_ref) * escape, axis=1, keepdims=True)


def density_of(news_ref, i, ne, slab):
    parts = []
    for z in range(ne):
        parts.append(jnp.transpose(news_ref[aligned(i * ne + z, TILE), :])[:slab])
    return jnp.concatenate(parts, 0)


def tables_kernel(ints_ref, source_ref, target_ref, rad_ref, pick_ref, move_ref, drain_ref):
    levels, total = pick_ref.shape
    step = min(512, total)
    acc = jnp.zeros((levels, levels), F32)
    ids = lax.broadcasted_iota(jnp.int32, (levels, step), 0)
    for at in range(0, total, step):
        src = ids == source_ref[0:1, at : at + step]
        tgt = ids == target_ref[0:1, at : at + step]
        pick = jnp.where(src, 1.0, 0.0)
        move = (jnp.where(tgt, 1.0, 0.0) - pick).astype(BF)
        pick_ref[:, at : at + step] = pick.astype(BF)
        move_ref[:, at : at + step] = move
        rad = rad_ref[0:1, at : at + step]
        high = rad.astype(BF).astype(F32)
        low = rad - high
        acc += dot_nt((pick * high).astype(BF), move)
        acc += dot_nt((pick * low).astype(BF), move)
    drain_ref[...] = acc


def scatter(pairs, k, rate_refs, pick_ref, move_ref, groups):
    rows = pairs.shape[0] // (2 * groups)
    part = rate_refs[0].shape[1]
    step = min(512, part)
    acc = jnp.zeros((pairs.shape[0], pick_ref.shape[0]), F32)
    for mask, ref in enumerate(rate_refs):
        for inner in range(0, part, step):
            at = pl.ds(pl.multiple_of((k ^ mask) * part + inner, step), step)
            rate = ref[:, inner : inner + step].astype(F32)
            picked = dot(pairs, pick_ref[:, at])
            parts = []
            for g in range(groups):
                own = picked[2 * g * rows : 2 * (g + 1) * rows]
                parts.append(halves(rate * fold(own)))
            flux = parts[0] if groups == 1 else jnp.concatenate(parts, 0)
            acc += dot_nt(flux, move_ref[:, at])
    return [fold(acc[2 * g * rows : 2 * (g + 1) * rows]) for g in range(groups)]


def drained(pairs, drain_ref):
    high, low = split(drain_ref[...])
    return fold(dot(pairs, high) + dot(pairs, low))


def first_kernel(block, ne):
    def kernel(ints_ref, level_ref, news_ref, owner_ref, partner_ref, pick_ref, move_ref, drain_ref, *refs):
        rates, (out_ref, told_ref) = refs[:ne], refs[ne:]
        k = ints_ref[0]
        levels = level_ref[...]
        escape = escape_of(news_ref, owner_ref, block)
        for _ in range(2):
            pairs = halves(levels)
            (moved,) = scatter(pairs, k, rates, pick_ref, move_ref, 1)
            levels = levels + level_step * (moved + escape * drained(pairs, drain_ref))
        out_ref[...] = levels
        put_news(levels, partner_ref, owner_ref, told_ref)

    return kernel


def second_kernel(ne):
    def kernel(ints_ref, level_ref, pick_ref, move_ref, drain_ref, *refs):
        rates, (c0_ref, c1_ref, c2_ref) = refs[:ne], refs[ne:]
        k = ints_ref[0]
        levels = level_ref[...]
        pairs = halves(levels)
        (moved,) = scatter(pairs, k, rates, pick_ref, move_ref, 1)
        u = levels + level_step * moved
        v = level_step * drained(pairs, drain_ref)
        pu, pv = halves(u), halves(v)
        mu, mv = scatter(jnp.concatenate([pu, pv], 0), k, rates, pick_ref, move_ref, 2)
        c0_ref[...] = u + level_step * mu
        c1_ref[...] = v + level_step * (mv + drained(pu, drain_ref))
        c2_ref[...] = level_step * drained(pv, drain_ref)

    return kernel


def final_kernel(block, ne, slab):
    def kernel(ints_ref, news_ref, owner_ref, c0_ref, c1_ref, c2_ref, current_ref, product_ref, out_ref, level_ref):
        escape = escape_of(news_ref, owner_ref, block)
        level_ref[...] = c0_ref[...] + escape * (c1_ref[...] + escape * c2_ref[...])
        density = density_of(news_ref, ints_ref[1], ne, slab)
        summed = density[:, 0:1] * product_ref[0]
        for p in range(1, product_ref.shape[0]):
            summed = summed + density[:, p : p + 1] * product_ref[p]
        out_ref[...] = current_ref[...] + boltz_step * summed

    return kernel


def place_spectra(ints_ref, spectra, row_ref):
    k = ints_ref[0]
    for mask, ref in enumerate(spectra):
        row_ref[:, aligned(k ^ mask, ref.shape[1])] = ref[...]


def product_of(ints_ref, row_ref, parts, p):
    total = None
    for n, ref in enumerate(parts):
        width = ref.shape[2]
        lhs = row_ref[...] if len(parts) == 1 else row_ref[:, aligned(ints_ref[2 + n], width)]
        term = dot_nt(lhs, ref[p])
        total = term if total is None else total + term
    return total


def first_product_kernel(ne, slab, count):
    def kernel(ints_ref, news_ref, *refs):
        spectra, parts, (current_ref, next_ref, row_ref) = refs[:ne], refs[ne : ne + count], refs[ne + count :]
        place_spectra(ints_ref, spectra, row_ref)
        density = density_of(news_ref, ints_ref[1], ne, slab)
        summed = None
        for p in range(parts[0].shape[0]):
            term = density[:, p : p + 1] * product_of(ints_ref, row_ref, parts, p)
            summed = term if summed is None else summed + term
        current = spectra[0][...].astype(F32) + boltz_step * summed
        current_ref[...] = current
        next_ref[...] = current.astype(BF)

    return kernel


def second_product_kernel(ne, count):
    def kernel(ints_ref, *refs):
        spectra, parts, (product_ref, row_ref) = refs[:ne], refs[ne : ne + count], refs[ne + count :]
        place_spectra(ints_ref, spectra, row_ref)
        for p in range(parts[0].shape[0]):
            product_ref[p] = product_of(ints_ref, row_ref, parts, p)

    return kernel


def rates_kernel(ne, count):
    def kernel(ints_ref, *refs):
        spectra, parts = refs[:ne], refs[ne : ne + count]
        outs, (row_ref, rate_ref) = refs[ne + count : 2 * ne + count], refs[2 * ne + count :]
        place_spectra(ints_ref, spectra, row_ref)
        row = row_ref[...]
        for n, ref in enumerate(parts):
            rates = jax.nn.softplus(dot_nt(row, ref[...])).astype(BF)
            if count == 1:
                rate_ref[...] = rates
            else:
                rate_ref[:, aligned(ints_ref[2 + n], ref.shape[0])] = rates
        for mask, out in enumerate(outs):
            out[...] = rate_ref[aligned(ints_ref[0] ^ mask, out.shape[0]), :]

    return kernel


def pack_kernel(ints_ref, *refs):
    place_spectra(ints_ref, refs[:-1], refs[-1])


def body(
    distribution,
    operators,
    sections,
    populations,
    cell_owner,
    partner_of,
    source,
    level_hop,
    radiative,
):
    nc = lax.axis_size("cells")
    ne = lax.axis_size("energy")
    i = lax.axis_index("cells")
    k = lax.axis_index("energy")
    slab, level_total = populations.shape
    block, width = distribution.shape
    partner_total, outs, _ = operators.shape
    reactions = source.shape[0]
    part = sections.shape[0] // ne
    small = nc == 8
    places = gathered_places(i) if small else [i]
    ints = jnp.stack([v.astype(jnp.int32) for v in [k, i] + places])

    def collect(x, axis):
        if small:
            return gather_cells(x)
        return [lax.all_gather(x, "cells", axis=axis, tiled=True)]

    def shared(news):
        return lax.all_to_all(news, ("cells", "energy"), 0, 0, tiled=True)

    news_shape = ((nc * ne * TILE, LANES), F32)
    partner_row = partner_of.reshape(1, level_total)

    operator_parts = collect(operators, 2)
    spectra = others(distribution, ne)
    shares = [lax.dynamic_slice_in_dim(sections, (k ^ m) * part, part, 0) for m in range(ne)]
    shares = [v if m == 0 else swap(v, "energy", m, ne) for m, v in enumerate(shares)]
    (news,) = call(news_kernel, [news_shape], ints, populations, partner_row, cell_owner)
    news = shared(news)
    (packed,) = call(pack_kernel, [((part, ne * width), BF)], ints, *shares)
    section_parts = collect(packed, 0)

    target = (source + level_hop) % level_total
    pick, move, drain = call(
        tables_kernel,
        [((level_total, reactions), BF)] * 2 + [((level_total, level_total), F32)],
        ints,
        *(
            jnp.swapaxes(v.reshape(nc, ne, part), 0, 1).reshape(1, reactions)
            for v in (source, target, radiative)
        ),
    )

    row = pltpu.VMEM((block, ne * width), BF)
    count = len(places)
    current, later = call(
        first_product_kernel(ne, slab, count),
        [((block, outs), F32), ((block, outs), BF)],
        ints,
        news,
        *spectra,
        *operator_parts,
        scratch=[row],
    )
    later = others(later, ne)

    def rates_of(chunks):
        rates = call(
            rates_kernel(ne, count),
            [((slab, nc * part), BF)] * ne,
            ints,
            *chunks,
            *section_parts,
            scratch=[row, pltpu.VMEM((block, nc * part), BF)],
        )
        got = {m: swap(rates[m], "energy", m, ne) for m in range(ne - 1, 0, -1)}
        return [rates[0]] + [got[m] for m in range(1, ne)]

    rates = rates_of(spectra)
    levels, news = call(
        first_kernel(block, ne),
        [(populations.shape, F32), news_shape],
        ints,
        populations,
        news,
        cell_owner,
        partner_row,
        pick,
        move,
        drain,
        *rates,
    )
    news = shared(news)
    rates = rates_of(later)
    (products,) = call(
        second_product_kernel(ne, count),
        [((partner_total, block, outs), F32)],
        ints,
        *later,
        *operator_parts,
        scratch=[row],
    )
    terms = call(
        second_kernel(ne), [(populations.shape, F32)] * 3, ints, levels, pick, move, drain, *rates
    )
    return call(
        final_kernel(block, ne, slab),
        [((block, outs), F32), (populations.shape, F32)],
        ints,
        news,
        cell_owner,
        *terms,
        current,
        products,
    )


def solution(mesh):
    return jax.shard_map(
        body,
        mesh=mesh,
        in_specs=(
            P("cells", "energy"),
            P(None, "energy", "cells"),
            P("cells", "energy"),
            P(("cells", "energy"), None),
            P(("cells", "energy"), None),
            P(),
            P(),
            P(),
            P(),
        ),
        out_specs=(P("cells", "energy"), P(("cells", "energy"), None)),
        check_vma=False,
    )
```

```python
import jax
import jax.numpy as jnp
from jax import lax
from jax.experimental import pallas as pl
from jax.experimental.pallas import tpu as pltpu
from jax.sharding import PartitionSpec as P

boltz_step = 0.5
level_step = 0.04
depth_scale = 2.0

BF = jnp.bfloat16
F32 = jnp.float32
NT = (((1,), (1,)), ((), ()))
TILE = 8
LANES = 128
COLUMN_ROW = 4
PARAMS = pltpu.CompilerParams(vmem_limit_bytes=24 << 20)


def swap(x, axis, mask, count):
    return lax.ppermute(x, axis, [(i, i ^ mask) for i in range(count)])


def others(x, ne):
    got = {mask: swap(x, "energy", mask, ne) for mask in range(ne - 1, 0, -1)}
    return [x] + [got[mask] for mask in range(1, ne)]


def cross(x, first):
    masks = (2, 4) if first else (4, 2)
    return lax.ppermute(x, "cells", [(i, i ^ masks[i & 1]) for i in range(8)])


def gathered_places(i):
    first = jnp.where((i & 1) == 0, 2, 4)
    own = [i, i ^ first, i ^ (6 - first), i ^ 6]
    sibling = [i ^ 1, i ^ 1 ^ (6 - first), i ^ 1 ^ first, i ^ 7]
    return own + sibling


def aligned(index, size):
    return pl.ds(pl.multiple_of(index * size, size), size)


def split(x):
    high = x.astype(BF)
    return high, (x - high.astype(F32)).astype(BF)


def halves(x):
    return jnp.concatenate(split(x), 0)


def dot(a, b):
    return jnp.dot(a, b, preferred_element_type=F32)


def dot_nt(a, b):
    return lax.dot_general(a, b, NT, preferred_element_type=F32)


def fold(x):
    n = x.shape[0] // 2
    return x[:n] + x[n:]


def call(kernel, shapes, ints, args, scratch=()):
    n, o = len(args), len(shapes)

    def whole(ints_ref, *refs):
        kernel(ints_ref, refs[:n], refs[n : n + o], refs[n + o :])

    return pl.pallas_call(
        whole,
        out_shape=tuple(jax.ShapeDtypeStruct(s, t) for s, t in shapes),
        in_specs=[pl.BlockSpec(memory_space=pltpu.SMEM)] + [pl.BlockSpec()] * n,
        scratch_shapes=list(scratch),
        compiler_params=PARAMS,
    )(ints, *args)


def after(x, *others):
    return lax.optimization_barrier((x,) + others)[0]


def zones_of(owner_ref):
    rows = owner_ref.shape[1]
    owner = owner_ref[...].astype(F32)
    if rows < LANES:
        owner = jnp.concatenate([owner, jnp.zeros((1, LANES - rows), F32)], 1)
    owner = jnp.transpose(jnp.broadcast_to(owner, (TILE, LANES)))[:rows, 0:1]
    lanes = lax.broadcasted_iota(jnp.int32, (rows, LANES), 1).astype(F32)
    return jnp.where(owner == lanes, 1.0, 0.0)


def news_of(levels, zones, partner_ref):
    rows, total = levels.shape
    ids = lax.broadcasted_iota(jnp.int32, (TILE, total), 0)
    chosen = jnp.where(ids == partner_ref[...], 1.0, 0.0)
    number = jnp.maximum(jnp.sum(chosen, axis=1, keepdims=True), 1.0)
    chosen = chosen.astype(BF)
    high, low = split(levels)
    density = (dot_nt(chosen, high) + dot_nt(chosen, low)) / number
    tile = jnp.concatenate([density, jnp.zeros((TILE, LANES - rows), F32)], 1)
    column = jnp.sum(zones * levels[:, 0:1], axis=0, keepdims=True)
    at = lax.broadcasted_iota(jnp.int32, (TILE, LANES), 0)
    return jnp.where(at == COLUMN_ROW, column, tile)


def message_kernel(ints_ref, args, outs, scratch):
    section_ref, level_ref, partner_ref, owner_ref = args
    k = ints_ref[0]
    news = halves(news_of(level_ref[...], zones_of(owner_ref), partner_ref))
    part = outs[0].shape[0] - 2 * TILE
    width = outs[0].shape[1]
    if width > LANES:
        news = jnp.concatenate([news, jnp.zeros((2 * TILE, width - LANES), BF)], 1)
    for mask, out in enumerate(outs):
        out[:part, :] = section_ref[aligned(k ^ mask, part), :]
        out[part:, :] = news


def pack_kernel(ints_ref, args, outs, scratch):
    packed_ref, news_ref = outs
    k = ints_ref[0]
    part = packed_ref.shape[0] - 2 * TILE
    total = None
    for mask, ref in enumerate(args):
        packed_ref[:part, aligned(k ^ mask, ref.shape[1])] = ref[:part, :]
        news = fold(ref[part:, :LANES].astype(F32))
        news_ref[aligned(k ^ mask, TILE), :] = news
        total = news if total is None else total + news
    packed_ref[part:, :] = jnp.concatenate(
        [halves(total), jnp.zeros((2 * TILE, packed_ref.shape[1] - LANES), BF)], 1
    )


def escape_of(column, zones, block):
    escape = 1.0 / (1.0 + depth_scale * column[COLUMN_ROW : COLUMN_ROW + 1] / block)
    return jnp.sum(zones * escape, axis=1, keepdims=True)


def density_of(news_ref, first, ne, slab):
    parts = []
    for z in range(ne):
        parts.append(jnp.transpose(news_ref[aligned(first + z, TILE), :])[:slab])
    return jnp.concatenate(parts, 0)


def tables_kernel(cells, energies):
    def kernel(ints_ref, args, outs, scratch):
        source_ref, hop_ref, rad_ref = args
        pick_ref, move_ref, drain_ref = outs
        chunks, levels, step = pick_ref.shape
        part = chunks * step // (cells * energies)
        starts = [c * energies * part + z * part for z in range(energies) for c in range(cells)]
        acc = jnp.zeros((levels, levels), F32)
        ids = lax.broadcasted_iota(jnp.int32, (levels, step), 0)
        each = step // part
        for n in range(chunks):

            def row(ref):
                pieces = [ref[0:1, at : at + part] for at in starts[n * each : (n + 1) * each]]
                return pieces[0] if each == 1 else jnp.concatenate(pieces, 1)

            source = row(source_ref)
            target = source + row(hop_ref)
            target = jnp.where(target >= levels, target - levels, target)
            pick = jnp.where(ids == source, 1.0, 0.0)
            move = (jnp.where(ids == target, 1.0, 0.0) - pick).astype(BF)
            pick_ref[n] = pick.astype(BF)
            move_ref[n] = move
            rad = row(rad_ref)
            high = rad.astype(BF).astype(F32)
            acc += dot_nt((pick * high).astype(BF), move)
            acc += dot_nt((pick * (rad - high)).astype(BF), move)
        drain_ref[...] = acc

    return kernel


def scatter(pairs, k, rate_refs, pick_ref, move_ref, groups):
    rows = pairs.shape[0] // (2 * groups)
    step = pick_ref.shape[2]
    acc = jnp.zeros(pairs.shape, F32)
    for mask, ref in enumerate(rate_refs):
        each = ref.shape[1] // step
        for inner in range(each):
            n = (k ^ mask) * each + inner
            rate = ref[:, inner * step : (inner + 1) * step].astype(F32)
            picked = dot(pairs, pick_ref[n])
            parts = []
            for g in range(groups):
                parts.append(halves(rate * fold(picked[2 * g * rows : 2 * (g + 1) * rows])))
            flux = parts[0] if groups == 1 else jnp.concatenate(parts, 0)
            acc += dot_nt(flux, move_ref[n])
    return [fold(acc[2 * g * rows : 2 * (g + 1) * rows]) for g in range(groups)]


def drained(pairs, drain_ref):
    high, low = split(drain_ref[...])
    return fold(dot(pairs, high) + dot(pairs, low))


def first_kernel(block):
    def kernel(ints_ref, args, outs, scratch):
        level_ref, column_ref, owner_ref, partner_ref, pick_ref, move_ref, drain_ref, *rates = args
        levels = level_ref[...]
        zones = zones_of(owner_ref)
        escape = escape_of(column_ref[...], zones, block)
        for _ in range(2):
            pairs = halves(levels)
            (moved,) = scatter(pairs, ints_ref[0], rates, pick_ref, move_ref, 1)
            levels = levels + level_step * (moved + escape * drained(pairs, drain_ref))
        outs[0][...] = levels
        news = news_of(levels, zones, partner_ref)
        for n in range(outs[1].shape[0] // TILE):
            outs[1][n * TILE : (n + 1) * TILE, :] = news

    return kernel


def second_kernel(ints_ref, args, outs, scratch):
    level_ref, pick_ref, move_ref, drain_ref, *rates = args
    k = ints_ref[0]
    levels = level_ref[...]
    pairs = halves(levels)
    (moved,) = scatter(pairs, k, rates, pick_ref, move_ref, 1)
    u = levels + level_step * moved
    v = level_step * drained(pairs, drain_ref)
    pu, pv = halves(u), halves(v)
    mu, mv = scatter(jnp.concatenate([pu, pv], 0), k, rates, pick_ref, move_ref, 2)
    outs[0][0] = u + level_step * mu
    outs[0][1] = v + level_step * (mv + drained(pu, drain_ref))
    outs[0][2] = level_step * drained(pv, drain_ref)


def final_kernel(block, ne, slab):
    def kernel(ints_ref, args, outs, scratch):
        news_ref, owner_ref, term_ref, current_ref, product_ref = args
        news = news_ref[...].reshape(news_ref.shape[0] // TILE, TILE, LANES)
        escape = escape_of(jnp.sum(news, axis=0), zones_of(owner_ref), block)
        outs[1][...] = term_ref[0] + escape * (term_ref[1] + escape * term_ref[2])
        density = density_of(news_ref, ints_ref[1] * ne, ne, slab)
        summed = density[:, 0:1] * product_ref[0]
        for p in range(1, product_ref.shape[0]):
            summed = summed + density[:, p : p + 1] * product_ref[p]
        outs[0][...] = current_ref[...] + boltz_step * summed

    return kernel


def place(ints_ref, parts, row_ref):
    for mask, ref in enumerate(parts):
        row_ref[:, aligned(ints_ref[0] ^ mask, ref.shape[1])] = ref[...]


def product_of(ints_ref, row_ref, parts, p):
    total = None
    for n, ref in enumerate(parts):
        width = ref.shape[2]
        lhs = row_ref[...] if len(parts) == 1 else row_ref[:, aligned(ints_ref[2 + n], width)]
        term = dot_nt(lhs, ref[p])
        total = term if total is None else total + term
    return total


def first_product_kernel(ne, slab):
    def kernel(ints_ref, args, outs, scratch):
        news_ref, *args = args
        spectra, parts, (row_ref,) = args[:ne], args[ne:], scratch
        place(ints_ref, spectra, row_ref)
        density = density_of(news_ref, 0, ne, slab)
        summed = None
        for p in range(parts[0].shape[0]):
            term = density[:, p : p + 1] * product_of(ints_ref, row_ref, parts, p)
            summed = term if summed is None else summed + term
        current = spectra[0][...].astype(F32) + boltz_step * summed
        outs[0][...] = current
        outs[1][...] = current.astype(BF)

    return kernel


def second_product_kernel(ne):
    def kernel(ints_ref, args, outs, scratch):
        place(ints_ref, args[:ne], scratch[0])
        for p in range(outs[0].shape[0]):
            outs[0][p] = product_of(ints_ref, scratch[0], args[ne:], p)

    return kernel


def rates_kernel(ne, small):
    def kernel(ints_ref, args, outs, scratch):
        spectra, parts, (row_ref, rate_ref) = args[:ne], args[ne:], scratch
        outs, column_ref = outs[:ne], outs[ne]
        place(ints_ref, spectra, row_ref)
        row = row_ref[...]
        column = None
        for n, ref in enumerate(parts):
            part = ref.shape[0] - 2 * TILE
            rates = jax.nn.softplus(dot_nt(row, ref[:part, :])).astype(BF)
            if small:
                rate_ref[:, aligned(ints_ref[2 + n], part)] = rates
            else:
                rate_ref[:, n * part : (n + 1) * part] = rates
            own = fold(ref[part:, :LANES].astype(F32))
            column = own if column is None else column + own
        column_ref[...] = column
        for mask, out in enumerate(outs):
            out[...] = rate_ref[aligned(ints_ref[0] ^ mask, out.shape[0]), :]

    return kernel


def body(
    distribution,
    operators,
    sections,
    populations,
    cell_owner,
    partner_of,
    source,
    level_hop,
    radiative,
):
    nc = lax.axis_size("cells")
    ne = lax.axis_size("energy")
    i = lax.axis_index("cells")
    k = lax.axis_index("energy")
    slab, level_total = populations.shape
    block, width = distribution.shape
    partner_total, outs, _ = operators.shape
    reactions = source.shape[0]
    part = sections.shape[0] // ne
    small = nc == 8
    places = gathered_places(i) if small else []
    ints = jnp.stack([v.astype(jnp.int32) for v in [k, i] + places])
    partner_row = partner_of.reshape(1, level_total)
    owner_row = cell_owner.reshape(1, slab)

    messages = call(
        message_kernel,
        [((part + 2 * TILE, width), BF)] * ne,
        ints,
        [sections, populations, partner_row, owner_row],
    )
    shares = {m: swap(messages[m], "energy", m, ne) for m in range(ne - 1, 0, -1)}
    spectra = others(distribution, ne)
    packed_shape = [((part + 2 * TILE, ne * width), BF), ((ne * TILE, LANES), F32)]
    packed_args = [messages[0]] + [shares[m] for m in range(1, ne)]
    if small:
        a, b = cross(operators, True), cross(operators, False)
        c = cross(b, True)
        own = swap(operators, "cells", 1, 8)
        packed_args[1] = after(packed_args[1], a, b, own)
        packed, density = call(pack_kernel, packed_shape, ints, packed_args)
        operator_parts = [operators, a, b, c, own] + [swap(v, "cells", 1, 8) for v in (a, b, c)]
        a, b = cross(packed, True), cross(packed, False)
        c = cross(after(b, operator_parts[3]), True)
        section_parts = [packed, a, b, c] + [swap(v, "cells", 1, 8) for v in (packed, a, b, c)]
    else:
        packed, density = call(pack_kernel, packed_shape, ints, packed_args)
        operator_parts = [lax.all_gather(operators, "cells", axis=2, tiled=True)]
        every = lax.all_gather(packed, "cells")
        section_parts = [every[n] for n in range(nc)]

    chunks = ((max(1, reactions // 512), level_total, min(512, reactions)), BF)
    pick, move, drain = call(
        tables_kernel(nc, ne),
        [chunks, chunks, ((level_total, level_total), F32)],
        ints,
        [v.reshape(1, reactions) for v in (source, level_hop, radiative)],
    )

    row = pltpu.VMEM((block, ne * width), BF)

    def rates_of(spectra):
        *rates, column = call(
            rates_kernel(ne, small),
            [((slab, nc * part), BF)] * ne + [((TILE, LANES), F32)],
            ints,
            list(spectra) + section_parts,
            [row, pltpu.VMEM((block, nc * part), BF)],
        )
        got = {m: swap(rates[m], "energy", m, ne) for m in range(ne - 1, 0, -1)}
        return [rates[0]] + [got[m] for m in range(1, ne)], column

    current, later = call(
        first_product_kernel(ne, slab),
        [((block, outs), F32), ((block, outs), BF)],
        ints,
        [density] + spectra + operator_parts,
        [row],
    )
    later = others(later, ne)
    rates, column = rates_of(spectra)
    (products,) = call(
        second_product_kernel(ne),
        [((partner_total, block, outs), F32)],
        ints,
        later + operator_parts,
        [row],
    )
    later_rates, _ = rates_of(later)
    rates[0] = after(rates[0], later_rates[0], products)
    levels, news = call(
        first_kernel(block),
        [(populations.shape, F32), ((nc * ne * TILE, LANES), F32)],
        ints,
        [populations, column, owner_row, partner_row, pick, move, drain] + rates,
    )
    news = lax.all_to_all(news, ("cells", "energy"), 0, 0, tiled=True)
    (terms,) = call(
        second_kernel,
        [((3,) + populations.shape, F32)],
        ints,
        [levels, pick, move, drain] + later_rates,
    )
    return call(
        final_kernel(block, ne, slab),
        [((block, outs), F32), (populations.shape, F32)],
        ints,
        [after(news, terms), owner_row, terms, current, products],
    )


def solution(mesh):
    return jax.shard_map(
        body,
        mesh=mesh,
        in_specs=(
            P("cells", "energy"),
            P(None, "energy", "cells"),
            P("cells", "energy"),
            P(("cells", "energy"), None),
            P(("cells", "energy"), None),
            P(),
            P(),
            P(),
            P(),
        ),
        out_specs=(P("cells", "energy"), P(("cells", "energy"), None)),
        check_vma=False,
    )
```

```python
import jax
import jax.numpy as jnp
from jax import lax
from jax.experimental import pallas as pl
from jax.experimental.pallas import tpu as pltpu
from jax.sharding import PartitionSpec as P

boltz_step = 0.5
level_step = 0.04
depth_scale = 2.0

BF = jnp.bfloat16
F32 = jnp.float32
NT = (((1,), (1,)), ((), ()))
TILE = 8
LANES = 128
COLUMN_ROW = 4
PARAMS = pltpu.CompilerParams(vmem_limit_bytes=24 << 20)


def swap(x, axis, mask, count):
    return lax.ppermute(x, axis, [(i, i ^ mask) for i in range(count)])


def others(x, ne):
    got = {mask: swap(x, "energy", mask, ne) for mask in range(ne - 1, 0, -1)}
    return [x] + [got[mask] for mask in range(1, ne)]


def chips(x):
    return [x] + [swap(x, "cells", mask, 8) for mask in (6, 2, 4)]


def siblings(own):
    return own + [swap(v, "cells", 1, 8) for v in own]


def gathered_places(i):
    return [i ^ mask for mask in (0, 6, 2, 4, 1, 7, 3, 5)]


def aligned(index, size):
    return pl.ds(pl.multiple_of(index * size, size), size)


def split(x):
    high = x.astype(BF)
    return high, (x - high.astype(F32)).astype(BF)


def halves(x):
    return jnp.concatenate(split(x), 0)


def dot(a, b):
    return jnp.dot(a, b, preferred_element_type=F32)


def dot_nt(a, b):
    return lax.dot_general(a, b, NT, preferred_element_type=F32)


def fold(x):
    n = x.shape[0] // 2
    return x[:n] + x[n:]


def call(kernel, shapes, ints, args, scratch=()):
    n, o = len(args), len(shapes)

    def whole(ints_ref, *refs):
        kernel(ints_ref, refs[:n], refs[n : n + o], refs[n + o :])

    return pl.pallas_call(
        whole,
        out_shape=tuple(jax.ShapeDtypeStruct(s, t) for s, t in shapes),
        in_specs=[pl.BlockSpec(memory_space=pltpu.SMEM)] + [pl.BlockSpec()] * n,
        scratch_shapes=list(scratch),
        compiler_params=PARAMS,
    )(ints, *args)


def after(x, *others):
    return lax.optimization_barrier((x,) + others)[0]


def zones_of(owner_ref):
    rows = owner_ref.shape[1]
    owner = owner_ref[...].astype(F32)
    if rows < LANES:
        owner = jnp.concatenate([owner, jnp.zeros((1, LANES - rows), F32)], 1)
    owner = jnp.transpose(jnp.broadcast_to(owner, (TILE, LANES)))[:rows, 0:1]
    lanes = lax.broadcasted_iota(jnp.int32, (rows, LANES), 1).astype(F32)
    return jnp.where(owner == lanes, 1.0, 0.0)


def news_of(levels, zones, partner_ref):
    rows, total = levels.shape
    ids = lax.broadcasted_iota(jnp.int32, (TILE, total), 0)
    chosen = jnp.where(ids == partner_ref[...], 1.0, 0.0)
    number = jnp.maximum(jnp.sum(chosen, axis=1, keepdims=True), 1.0)
    chosen = chosen.astype(BF)
    high, low = split(levels)
    density = (dot_nt(chosen, high) + dot_nt(chosen, low)) / number
    tile = jnp.concatenate([density, jnp.zeros((TILE, LANES - rows), F32)], 1)
    column = jnp.sum(zones * levels[:, 0:1], axis=0, keepdims=True)
    at = lax.broadcasted_iota(jnp.int32, (TILE, LANES), 0)
    return jnp.where(at == COLUMN_ROW, column, tile)


def message_kernel(ints_ref, args, outs, scratch):
    spectra_ref, section_ref, level_ref, partner_ref, owner_ref = args
    block = spectra_ref.shape[0]
    k = ints_ref[0]
    news = halves(news_of(level_ref[...], zones_of(owner_ref), partner_ref))
    part = outs[0].shape[0] - 2 * TILE - block
    width = outs[0].shape[1]
    if width > LANES:
        news = jnp.concatenate([news, jnp.zeros((2 * TILE, width - LANES), BF)], 1)
    for mask, out in enumerate(outs):
        out[:block, :] = spectra_ref[...]
        out[block : block + part, :] = section_ref[aligned(k ^ mask, part), :]
        out[block + part :, :] = news


def pack_kernel(ints_ref, args, outs, scratch):
    packed_ref, news_ref = outs
    k = ints_ref[0]
    part = packed_ref.shape[0] - 2 * TILE
    total = None
    for mask, ref in enumerate(args):
        below = ref.shape[0] - 2 * TILE
        packed_ref[:part, aligned(k ^ mask, ref.shape[1])] = ref[below - part : below, :]
        news = fold(ref[below:, :LANES].astype(F32))
        news_ref[aligned(k ^ mask, TILE), :] = news
        total = news if total is None else total + news
    packed_ref[part:, :] = jnp.concatenate(
        [halves(total), jnp.zeros((2 * TILE, packed_ref.shape[1] - LANES), BF)], 1
    )


def escape_of(column, zones, block):
    escape = 1.0 / (1.0 + depth_scale * column[COLUMN_ROW : COLUMN_ROW + 1] / block)
    return jnp.sum(zones * escape, axis=1, keepdims=True)


def density_of(news_ref, first, ne, slab):
    parts = []
    for z in range(ne):
        parts.append(jnp.transpose(news_ref[aligned(first + z, TILE), :])[:slab])
    return jnp.concatenate(parts, 0)


def tables_kernel(cells, energies):
    def kernel(ints_ref, args, outs, scratch):
        source_ref, hop_ref, rad_ref = args
        pick_ref, move_ref, drain_ref = outs
        chunks, levels, step = pick_ref.shape
        part = chunks * step // (cells * energies)
        starts = [c * energies * part + z * part for z in range(energies) for c in range(cells)]
        acc = jnp.zeros((levels, levels), F32)
        ids = lax.broadcasted_iota(jnp.int32, (levels, step), 0)
        each = step // part
        for n in range(chunks):

            def row(ref):
                pieces = [ref[0:1, at : at + part] for at in starts[n * each : (n + 1) * each]]
                return pieces[0] if each == 1 else jnp.concatenate(pieces, 1)

            source = row(source_ref)
            target = source + row(hop_ref)
            target = jnp.where(target >= levels, target - levels, target)
            pick = jnp.where(ids == source, 1.0, 0.0)
            move = (jnp.where(ids == target, 1.0, 0.0) - pick).astype(BF)
            pick_ref[n] = pick.astype(BF)
            move_ref[n] = move
            rad = row(rad_ref)
            high = rad.astype(BF).astype(F32)
            acc += dot_nt((pick * high).astype(BF), move)
            acc += dot_nt((pick * (rad - high)).astype(BF), move)
        drain_ref[...] = acc

    return kernel


def scatter(pairs, k, rate_refs, pick_ref, move_ref, groups):
    rows = pairs.shape[0] // (2 * groups)
    step = pick_ref.shape[2]
    acc = jnp.zeros(pairs.shape, F32)
    for mask, ref in enumerate(rate_refs):
        each = ref.shape[1] // step
        for inner in range(each):
            n = (k ^ mask) * each + inner
            rate = ref[:, inner * step : (inner + 1) * step].astype(F32)
            picked = dot(pairs, pick_ref[n])
            parts = []
            for g in range(groups):
                parts.append(halves(rate * fold(picked[2 * g * rows : 2 * (g + 1) * rows])))
            flux = parts[0] if groups == 1 else jnp.concatenate(parts, 0)
            acc += dot_nt(flux, move_ref[n])
    return [fold(acc[2 * g * rows : 2 * (g + 1) * rows]) for g in range(groups)]


def drained(pairs, drain_ref):
    high, low = split(drain_ref[...])
    return fold(dot(pairs, high) + dot(pairs, low))


def first_kernel(block):
    def kernel(ints_ref, args, outs, scratch):
        level_ref, column_ref, owner_ref, partner_ref, pick_ref, move_ref, drain_ref, *rates = args
        levels = level_ref[...]
        zones = zones_of(owner_ref)
        escape = escape_of(column_ref[...], zones, block)
        for _ in range(2):
            pairs = halves(levels)
            (moved,) = scatter(pairs, ints_ref[0], rates, pick_ref, move_ref, 1)
            levels = levels + level_step * (moved + escape * drained(pairs, drain_ref))
        outs[0][...] = levels
        outs[1][...] = news_of(levels, zones, partner_ref)

    return kernel


def second_kernel(ints_ref, args, outs, scratch):
    level_ref, pick_ref, move_ref, drain_ref, *rates = args
    k = ints_ref[0]
    levels = level_ref[...]
    pairs = halves(levels)
    (moved,) = scatter(pairs, k, rates, pick_ref, move_ref, 1)
    u = levels + level_step * moved
    v = level_step * drained(pairs, drain_ref)
    pu, pv = halves(u), halves(v)
    mu, mv = scatter(jnp.concatenate([pu, pv], 0), k, rates, pick_ref, move_ref, 2)
    outs[0][0] = u + level_step * mu
    outs[0][1] = v + level_step * (mv + drained(pu, drain_ref))
    outs[0][2] = level_step * drained(pv, drain_ref)


def final_kernel(block, ne, slab):
    def kernel(ints_ref, args, outs, scratch):
        owner_ref, term_ref, current_ref, product_ref, *tiles = args
        (news_ref,) = scratch
        for mask, ref in enumerate(tiles[:ne]):
            news_ref[aligned(ints_ref[0] ^ mask, TILE), :] = ref[...]
        column = tiles[ne][...]
        for ref in tiles[ne + 1 :]:
            column = column + ref[...]
        escape = escape_of(column, zones_of(owner_ref), block)
        outs[1][...] = term_ref[0] + escape * (term_ref[1] + escape * term_ref[2])
        density = density_of(news_ref, 0, ne, slab)
        summed = density[:, 0:1] * product_ref[0]
        for p in range(1, product_ref.shape[0]):
            summed = summed + density[:, p : p + 1] * product_ref[p]
        outs[0][...] = current_ref[...] + boltz_step * summed

    return kernel


def place(ints_ref, parts, row_ref):
    for mask, ref in enumerate(parts):
        row_ref[:, aligned(ints_ref[0] ^ mask, ref.shape[1])] = ref[: row_ref.shape[0], :]


def product_of(ints_ref, row_ref, parts, p):
    total = None
    for n, ref in enumerate(parts):
        width = ref.shape[2]
        lhs = row_ref[...] if len(parts) == 1 else row_ref[:, aligned(ints_ref[2 + n], width)]
        term = dot_nt(lhs, ref[p])
        total = term if total is None else total + term
    return total


def first_product_kernel(ne, slab):
    def kernel(ints_ref, args, outs, scratch):
        news_ref, *args = args
        spectra, parts, (row_ref,) = args[:ne], args[ne:], scratch
        place(ints_ref, spectra, row_ref)
        density = density_of(news_ref, 0, ne, slab)
        summed = None
        for p in range(parts[0].shape[0]):
            term = density[:, p : p + 1] * product_of(ints_ref, row_ref, parts, p)
            summed = term if summed is None else summed + term
        current = spectra[0][: row_ref.shape[0], :].astype(F32) + boltz_step * summed
        outs[0][...] = current
        outs[1][...] = current.astype(BF)

    return kernel


def second_product_kernel(ne):
    def kernel(ints_ref, args, outs, scratch):
        place(ints_ref, args[:ne], scratch[0])
        for p in range(outs[0].shape[0]):
            outs[0][p] = product_of(ints_ref, scratch[0], args[ne:], p)

    return kernel


def rates_kernel(ne, small):
    def kernel(ints_ref, args, outs, scratch):
        spectra, parts, (row_ref, rate_ref) = args[:ne], args[ne:], scratch
        outs, column_ref = outs[:ne], outs[ne]
        place(ints_ref, spectra, row_ref)
        row = row_ref[...]
        column = None
        for n, ref in enumerate(parts):
            part = ref.shape[0] - 2 * TILE
            rates = jax.nn.softplus(dot_nt(row, ref[:part, :])).astype(BF)
            if small:
                rate_ref[:, aligned(ints_ref[2 + n], part)] = rates
            else:
                rate_ref[:, n * part : (n + 1) * part] = rates
            own = fold(ref[part:, :LANES].astype(F32))
            column = own if column is None else column + own
        column_ref[...] = column
        for mask, out in enumerate(outs):
            out[...] = rate_ref[aligned(ints_ref[0] ^ mask, out.shape[0]), :]

    return kernel


def body(
    distribution,
    operators,
    sections,
    populations,
    cell_owner,
    partner_of,
    source,
    level_hop,
    radiative,
):
    nc = lax.axis_size("cells")
    ne = lax.axis_size("energy")
    i = lax.axis_index("cells")
    k = lax.axis_index("energy")
    slab, level_total = populations.shape
    block, width = distribution.shape
    partner_total, outs, _ = operators.shape
    reactions = source.shape[0]
    part = sections.shape[0] // ne
    small = nc == 8
    places = gathered_places(i) if small else []
    ints = jnp.stack([v.astype(jnp.int32) for v in [k, i] + places])
    partner_row = partner_of.reshape(1, level_total)
    owner_row = cell_owner.reshape(1, slab)

    messages = call(
        message_kernel,
        [((block + part + 2 * TILE, width), BF)] * ne,
        ints,
        [distribution, sections, populations, partner_row, owner_row],
    )
    got = {m: swap(messages[m], "energy", m, ne) for m in range(ne - 1, 0, -1)}
    spectra = [messages[0]] + [got[m] for m in range(1, ne)]
    packed_shape = [((part + 2 * TILE, ne * width), BF), ((ne * TILE, LANES), F32)]
    packed_args = list(spectra)
    if small:
        operator_parts = chips(operators)
        packed_args[1] = after(packed_args[1], *operator_parts[1:])
        packed, density = call(pack_kernel, packed_shape, ints, packed_args)
        operator_parts = siblings(operator_parts)
        section_parts = chips(packed)
    else:
        packed, density = call(pack_kernel, packed_shape, ints, packed_args)
        operator_parts = [lax.all_gather(operators, "cells", axis=2, tiled=True)]
        every = lax.all_gather(packed, "cells")
        section_parts = [every[n] for n in range(nc)]

    chunks = ((max(1, reactions // 512), level_total, min(512, reactions)), BF)
    pick, move, drain = call(
        tables_kernel(nc, ne),
        [chunks, chunks, ((level_total, level_total), F32)],
        ints,
        [v.reshape(1, reactions) for v in (source, level_hop, radiative)],
    )

    row = pltpu.VMEM((block, ne * width), BF)

    current, later = call(
        first_product_kernel(ne, slab),
        [((block, outs), F32), ((block, outs), BF)],
        ints,
        [density] + spectra + operator_parts,
        [row],
    )
    later = others(later, ne)
    if small:
        section_parts = siblings(section_parts[:1] + [after(v, later[1], later[2]) for v in section_parts[1:]])

    def rates_of(spectra):
        *rates, column = call(
            rates_kernel(ne, small),
            [((slab, nc * part), BF)] * ne + [((TILE, LANES), F32)],
            ints,
            list(spectra) + section_parts,
            [row, pltpu.VMEM((block, nc * part), BF)],
        )
        got = {m: swap(rates[m], "energy", m, ne) for m in range(ne - 1, 0, -1)}
        return [rates[0]] + [got[m] for m in range(1, ne)], column

    rates, column = rates_of(spectra)
    (products,) = call(
        second_product_kernel(ne),
        [((partner_total, block, outs), F32)],
        ints,
        later + operator_parts,
        [row],
    )
    later_rates, _ = rates_of(later)
    rates[0] = after(rates[0], later_rates[0], products)
    levels, news = call(
        first_kernel(block),
        [(populations.shape, F32), ((TILE, LANES), F32)],
        ints,
        [populations, column, owner_row, partner_row, pick, move, drain] + rates,
    )
    if small:
        row_of = lax.broadcasted_iota(jnp.int32, (TILE, LANES), 0)
        news = after(news, later_rates[1])
        news = news + jnp.where(row_of == COLUMN_ROW, swap(news, "cells", 1, nc), 0.0)
    news = others(news, ne)
    column = sum(news[1:], news[0])
    columns = chips(column) if small else [lax.psum(column, "cells")]
    (terms,) = call(
        second_kernel,
        [((3,) + populations.shape, F32)],
        ints,
        [levels, pick, move, drain] + later_rates,
    )
    return call(
        final_kernel(block, ne, slab),
        [((block, outs), F32), (populations.shape, F32)],
        ints,
        [owner_row, terms, current, products] + news + columns,
        [pltpu.VMEM((ne * TILE, LANES), F32)],
    )


def solution(mesh):
    return jax.shard_map(
        body,
        mesh=mesh,
        in_specs=(
            P("cells", "energy"),
            P(None, "energy", "cells"),
            P("cells", "energy"),
            P(("cells", "energy"), None),
            P(("cells", "energy"), None),
            P(),
            P(),
            P(),
            P(),
        ),
        out_specs=(P("cells", "energy"), P(("cells", "energy"), None)),
        check_vma=False,
    )
```

```python
import jax
import jax.numpy as jnp
from jax import lax
from jax.experimental import pallas as pl
from jax.experimental.pallas import tpu as pltpu
from jax.sharding import PartitionSpec as P

boltz_step = 0.5
level_step = 0.04
depth_scale = 2.0

BF = jnp.bfloat16
F32 = jnp.float32
NT = (((1,), (1,)), ((), ()))
TILE = 8
LANES = 128
COLUMN_ROW = 4
PARAMS = pltpu.CompilerParams(vmem_limit_bytes=24 << 20)


def swap(x, axis, mask, count):
    return lax.ppermute(x, axis, [(i, i ^ mask) for i in range(count)])


def others(x, ne):
    got = {mask: swap(x, "energy", mask, ne) for mask in range(ne - 1, 0, -1)}
    return [x] + [got[mask] for mask in range(1, ne)]


def chips(x):
    return [x] + [swap(x, "cells", mask, 8) for mask in (6, 2, 4)]


def siblings(own):
    return own + [swap(v, "cells", 1, 8) for v in own]


def gathered_places(i):
    return [i ^ mask for mask in (0, 6, 2, 4, 1, 7, 3, 5)]


def aligned(index, size):
    return pl.ds(pl.multiple_of(index * size, size), size)


def split(x):
    high = x.astype(BF)
    return high, (x - high.astype(F32)).astype(BF)


def halves(x):
    return jnp.concatenate(split(x), 0)


def dot(a, b):
    return jnp.dot(a, b, preferred_element_type=F32)


def dot_nt(a, b):
    return lax.dot_general(a, b, NT, preferred_element_type=F32)


def fold(x):
    n = x.shape[0] // 2
    return x[:n] + x[n:]


def call(kernel, shapes, ints, args, scratch=()):
    n, o = len(args), len(shapes)

    def whole(ints_ref, *refs):
        kernel(ints_ref, refs[:n], refs[n : n + o], refs[n + o :])

    return pl.pallas_call(
        whole,
        out_shape=tuple(jax.ShapeDtypeStruct(s, t) for s, t in shapes),
        in_specs=[pl.BlockSpec(memory_space=pltpu.SMEM)] + [pl.BlockSpec()] * n,
        scratch_shapes=list(scratch),
        compiler_params=PARAMS,
    )(ints, *args)


def after(x, *others):
    return lax.optimization_barrier((x,) + others)[0]


def zones_of(owner_ref):
    rows = owner_ref.shape[1]
    owner = owner_ref[...].astype(F32)
    if rows < LANES:
        owner = jnp.concatenate([owner, jnp.zeros((1, LANES - rows), F32)], 1)
    owner = jnp.transpose(jnp.broadcast_to(owner, (TILE, LANES)))[:rows, 0:1]
    lanes = lax.broadcasted_iota(jnp.int32, (rows, LANES), 1).astype(F32)
    return jnp.where(owner == lanes, 1.0, 0.0)


def news_of(levels, zones, partner_ref):
    rows, total = levels.shape
    ids = lax.broadcasted_iota(jnp.int32, (TILE, total), 0)
    chosen = jnp.where(ids == partner_ref[...], 1.0, 0.0)
    number = jnp.maximum(jnp.sum(chosen, axis=1, keepdims=True), 1.0)
    chosen = chosen.astype(BF)
    high, low = split(levels)
    density = (dot_nt(chosen, high) + dot_nt(chosen, low)) / number
    tile = jnp.concatenate([density, jnp.zeros((TILE, LANES - rows), F32)], 1)
    column = jnp.sum(zones * levels[:, 0:1], axis=0, keepdims=True)
    at = lax.broadcasted_iota(jnp.int32, (TILE, LANES), 0)
    return jnp.where(at == COLUMN_ROW, column, tile)


def message_kernel(ints_ref, args, outs, scratch):
    spectra_ref, section_ref, level_ref, partner_ref, owner_ref = args
    block = spectra_ref.shape[0]
    k = ints_ref[0]
    news = halves(news_of(level_ref[...], zones_of(owner_ref), partner_ref))
    part = outs[0].shape[0] - 2 * TILE - block
    width = outs[0].shape[1]
    if width > LANES:
        news = jnp.concatenate([news, jnp.zeros((2 * TILE, width - LANES), BF)], 1)
    for mask, out in enumerate(outs):
        out[:block, :] = spectra_ref[...]
        out[block : block + part, :] = section_ref[aligned(k ^ mask, part), :]
        out[block + part :, :] = news


def pack_kernel(ints_ref, args, outs, scratch):
    packed_ref, news_ref = outs
    k = ints_ref[0]
    part = packed_ref.shape[0] - 2 * TILE
    total = None
    for mask, ref in enumerate(args):
        below = ref.shape[0] - 2 * TILE
        packed_ref[:part, aligned(k ^ mask, ref.shape[1])] = ref[below - part : below, :]
        news = fold(ref[below:, :LANES].astype(F32))
        news_ref[aligned(k ^ mask, TILE), :] = news
        total = news if total is None else total + news
    packed_ref[part:, :] = jnp.concatenate(
        [halves(total), jnp.zeros((2 * TILE, packed_ref.shape[1] - LANES), BF)], 1
    )


def escape_of(column, zones, block):
    escape = 1.0 / (1.0 + depth_scale * column[COLUMN_ROW : COLUMN_ROW + 1] / block)
    return jnp.sum(zones * escape, axis=1, keepdims=True)


def density_of(news_ref, first, ne, slab):
    parts = []
    for z in range(ne):
        parts.append(jnp.transpose(news_ref[aligned(first + z, TILE), :])[:slab])
    return jnp.concatenate(parts, 0)


def tables_kernel(cells, energies):
    def kernel(ints_ref, args, outs, scratch):
        source_ref, hop_ref, rad_ref = args
        pick_ref, move_ref, drain_ref = outs
        chunks, levels, step = pick_ref.shape
        part = chunks * step // (cells * energies)
        starts = [c * energies * part + z * part for z in range(energies) for c in range(cells)]
        acc = jnp.zeros((levels, levels), F32)
        ids = lax.broadcasted_iota(jnp.int32, (levels, step), 0)
        each = step // part
        for n in range(chunks):

            def row(ref):
                pieces = [ref[0:1, at : at + part] for at in starts[n * each : (n + 1) * each]]
                return pieces[0] if each == 1 else jnp.concatenate(pieces, 1)

            source = row(source_ref)
            target = source + row(hop_ref)
            target = jnp.where(target >= levels, target - levels, target)
            pick = jnp.where(ids == source, 1.0, 0.0)
            move = (jnp.where(ids == target, 1.0, 0.0) - pick).astype(BF)
            pick_ref[n] = pick.astype(BF)
            move_ref[n] = move
            rad = row(rad_ref)
            high = rad.astype(BF).astype(F32)
            acc += dot_nt((pick * high).astype(BF), move)
            acc += dot_nt((pick * (rad - high)).astype(BF), move)
        drain_ref[...] = acc

    return kernel


def scatter(pairs, k, rate_refs, pick_ref, move_ref, groups):
    rows = pairs.shape[0] // (2 * groups)
    step = pick_ref.shape[2]
    acc = jnp.zeros(pairs.shape, F32)
    for mask, ref in enumerate(rate_refs):
        each = ref.shape[1] // step
        for inner in range(each):
            n = (k ^ mask) * each + inner
            rate = ref[:, inner * step : (inner + 1) * step].astype(F32)
            picked = dot(pairs, pick_ref[n])
            parts = []
            for g in range(groups):
                parts.append(halves(rate * fold(picked[2 * g * rows : 2 * (g + 1) * rows])))
            flux = parts[0] if groups == 1 else jnp.concatenate(parts, 0)
            acc += dot_nt(flux, move_ref[n])
    return [fold(acc[2 * g * rows : 2 * (g + 1) * rows]) for g in range(groups)]


def drained(pairs, drain_ref):
    high, low = split(drain_ref[...])
    return fold(dot(pairs, high) + dot(pairs, low))


def first_kernel(block):
    def kernel(ints_ref, args, outs, scratch):
        level_ref, column_ref, owner_ref, partner_ref, pick_ref, move_ref, drain_ref, *rates = args
        levels = level_ref[...]
        zones = zones_of(owner_ref)
        escape = escape_of(column_ref[...], zones, block)
        for _ in range(2):
            pairs = halves(levels)
            (moved,) = scatter(pairs, ints_ref[0], rates, pick_ref, move_ref, 1)
            levels = levels + level_step * (moved + escape * drained(pairs, drain_ref))
        outs[0][...] = levels
        outs[1][...] = news_of(levels, zones, partner_ref)

    return kernel


def second_kernel(ints_ref, args, outs, scratch):
    level_ref, pick_ref, move_ref, drain_ref, *rates = args
    k = ints_ref[0]
    levels = level_ref[...]
    pairs = halves(levels)
    (moved,) = scatter(pairs, k, rates, pick_ref, move_ref, 1)
    u = levels + level_step * moved
    v = level_step * drained(pairs, drain_ref)
    pu, pv = halves(u), halves(v)
    mu, mv = scatter(jnp.concatenate([pu, pv], 0), k, rates, pick_ref, move_ref, 2)
    outs[0][0] = u + level_step * mu
    outs[0][1] = v + level_step * (mv + drained(pu, drain_ref))
    outs[0][2] = level_step * drained(pv, drain_ref)


def final_kernel(block, ne, slab):
    def kernel(ints_ref, args, outs, scratch):
        owner_ref, term_ref, current_ref, product_ref, *tiles = args
        (news_ref,) = scratch
        for mask, ref in enumerate(tiles[:ne]):
            news_ref[aligned(ints_ref[0] ^ mask, TILE), :] = ref[...]
        column = tiles[ne][...]
        for ref in tiles[ne + 1 :]:
            column = column + ref[...]
        escape = escape_of(column, zones_of(owner_ref), block)
        outs[1][...] = term_ref[0] + escape * (term_ref[1] + escape * term_ref[2])
        density = density_of(news_ref, 0, ne, slab)
        summed = density[:, 0:1] * product_ref[0]
        for p in range(1, product_ref.shape[0]):
            summed = summed + density[:, p : p + 1] * product_ref[p]
        outs[0][...] = current_ref[...] + boltz_step * summed

    return kernel


def place(ints_ref, parts, row_ref):
    for mask, ref in enumerate(parts):
        row_ref[:, aligned(ints_ref[0] ^ mask, ref.shape[1])] = ref[: row_ref.shape[0], :]


def product_of(ints_ref, row_ref, parts, p):
    total = None
    for n, ref in enumerate(parts):
        width = ref.shape[2]
        lhs = row_ref[...] if len(parts) == 1 else row_ref[:, aligned(ints_ref[2 + n], width)]
        term = dot_nt(lhs, ref[p])
        total = term if total is None else total + term
    return total


def first_product_kernel(ne, slab):
    def kernel(ints_ref, args, outs, scratch):
        news_ref, *args = args
        spectra, parts, (row_ref,) = args[:ne], args[ne:], scratch
        place(ints_ref, spectra, row_ref)
        density = density_of(news_ref, 0, ne, slab)
        summed = None
        for p in range(parts[0].shape[0]):
            term = density[:, p : p + 1] * product_of(ints_ref, row_ref, parts, p)
            summed = term if summed is None else summed + term
        current = spectra[0][: row_ref.shape[0], :].astype(F32) + boltz_step * summed
        outs[0][...] = current
        outs[1][...] = current.astype(BF)

    return kernel


def second_product_kernel(ne):
    def kernel(ints_ref, args, outs, scratch):
        place(ints_ref, args[:ne], scratch[0])
        for p in range(outs[0].shape[0]):
            outs[0][p] = product_of(ints_ref, scratch[0], args[ne:], p)

    return kernel


def rates_kernel(ne, small):
    def kernel(ints_ref, args, outs, scratch):
        spectra, parts, (row_ref, rate_ref) = args[:ne], args[ne:], scratch
        outs, column_ref = outs[:ne], outs[ne]
        place(ints_ref, spectra, row_ref)
        row = row_ref[...]
        column = None
        for n, ref in enumerate(parts):
            part = ref.shape[0] - 2 * TILE
            rates = jax.nn.softplus(dot_nt(row, ref[:part, :])).astype(BF)
            if small:
                rate_ref[:, aligned(ints_ref[2 + n], part)] = rates
            else:
                rate_ref[:, n * part : (n + 1) * part] = rates
            own = fold(ref[part:, :LANES].astype(F32))
            column = own if column is None else column + own
        column_ref[...] = column
        for mask, out in enumerate(outs):
            out[...] = rate_ref[aligned(ints_ref[0] ^ mask, out.shape[0]), :]

    return kernel


def body(
    distribution,
    operators,
    sections,
    populations,
    cell_owner,
    partner_of,
    source,
    level_hop,
    radiative,
):
    nc = lax.axis_size("cells")
    ne = lax.axis_size("energy")
    i = lax.axis_index("cells")
    k = lax.axis_index("energy")
    slab, level_total = populations.shape
    block, width = distribution.shape
    partner_total, outs, _ = operators.shape
    reactions = source.shape[0]
    part = sections.shape[0] // ne
    small = nc == 8
    places = gathered_places(i) if small else []
    ints = jnp.stack([v.astype(jnp.int32) for v in [k, i] + places])
    partner_row = partner_of.reshape(1, level_total)
    owner_row = cell_owner.reshape(1, slab)

    messages = call(
        message_kernel,
        [((block + part + 2 * TILE, width), BF)] * ne,
        ints,
        [distribution, sections, populations, partner_row, owner_row],
    )
    got = {m: swap(messages[m], "energy", m, ne) for m in range(ne - 1, 0, -1)}
    spectra = [messages[0]] + [got[m] for m in range(1, ne)]
    packed_shape = [((part + 2 * TILE, ne * width), BF), ((ne * TILE, LANES), F32)]
    packed_args = list(spectra)
    if small:
        operator_parts = chips(operators)
        packed_args[1] = after(packed_args[1], *operator_parts[1:])
        packed, density = call(pack_kernel, packed_shape, ints, packed_args)
        operator_parts = siblings(operator_parts)
        section_parts = chips(packed)
    else:
        packed, density = call(pack_kernel, packed_shape, ints, packed_args)
        operator_parts = [lax.all_gather(operators, "cells", axis=2, tiled=True)]
        every = lax.all_gather(packed, "cells")
        section_parts = [every[n] for n in range(nc)]

    chunks = ((max(1, reactions // 512), level_total, min(512, reactions)), BF)
    pick, move, drain = call(
        tables_kernel(nc, ne),
        [chunks, chunks, ((level_total, level_total), F32)],
        ints,
        [v.reshape(1, reactions) for v in (source, level_hop, radiative)],
    )

    row = pltpu.VMEM((block, ne * width), BF)

    current, later = call(
        first_product_kernel(ne, slab),
        [((block, outs), F32), ((block, outs), BF)],
        ints,
        [density] + spectra + operator_parts,
        [row],
    )
    later = others(later, ne)
    if small:
        section_parts = siblings(section_parts[:1] + [after(v, later[1], later[2]) for v in section_parts[1:]])

    def rates_of(spectra):
        *rates, column = call(
            rates_kernel(ne, small),
            [((slab, nc * part), BF)] * ne + [((TILE, LANES), F32)],
            ints,
            list(spectra) + section_parts,
            [row, pltpu.VMEM((block, nc * part), BF)],
        )
        got = {m: swap(rates[m], "energy", m, ne) for m in range(ne - 1, 0, -1)}
        return [rates[0]] + [got[m] for m in range(1, ne)], column

    rates, column = rates_of(spectra)
    (products,) = call(
        second_product_kernel(ne),
        [((partner_total, block, outs), F32)],
        ints,
        later + operator_parts,
        [row],
    )
    later_rates, _ = rates_of(later)
    rates[0] = after(rates[0], later_rates[0], products)
    levels, news = call(
        first_kernel(block),
        [(populations.shape, F32), ((TILE, LANES), F32)],
        ints,
        [populations, column, owner_row, partner_row, pick, move, drain] + rates,
    )
    if small:
        row_of = lax.broadcasted_iota(jnp.int32, (TILE, LANES), 0)
        news = after(news, later_rates[1], later_rates[2])
        news = news + jnp.where(row_of == COLUMN_ROW, swap(news, "cells", 1, nc), 0.0)
    news = others(news, ne)
    column = sum(news[1:], news[0])
    columns = chips(column) if small else [lax.psum(column, "cells")]
    (terms,) = call(
        second_kernel,
        [((3,) + populations.shape, F32)],
        ints,
        [levels, pick, move, drain] + later_rates,
    )
    return call(
        final_kernel(block, ne, slab),
        [((block, outs), F32), (populations.shape, F32)],
        ints,
        [owner_row, terms, current, products] + news + columns,
        [pltpu.VMEM((ne * TILE, LANES), F32)],
    )


def solution(mesh):
    return jax.shard_map(
        body,
        mesh=mesh,
        in_specs=(
            P("cells", "energy"),
            P(None, "energy", "cells"),
            P("cells", "energy"),
            P(("cells", "energy"), None),
            P(("cells", "energy"), None),
            P(),
            P(),
            P(),
            P(),
        ),
        out_specs=(P("cells", "energy"), P(("cells", "energy"), None)),
        check_vma=False,
    )
```

```python
import jax
import jax.numpy as jnp
from jax import lax
from jax.experimental import pallas as pl
from jax.experimental.pallas import tpu as pltpu
from jax.sharding import PartitionSpec as P

boltz_step = 0.5
level_step = 0.04
depth_scale = 2.0

BF = jnp.bfloat16
F32 = jnp.float32
NT = (((1,), (1,)), ((), ()))
TILE = 8
LANES = 128
COLUMN_ROW = 4
PARAMS = pltpu.CompilerParams(vmem_limit_bytes=24 << 20)


def swap(x, axis, mask, count):
    return lax.ppermute(x, axis, [(i, i ^ mask) for i in range(count)])


def others(x, ne):
    got = {mask: swap(x, "energy", mask, ne) for mask in range(ne - 1, 0, -1)}
    return [x] + [got[mask] for mask in range(1, ne)]


def chips(x):
    return [x] + [swap(x, "cells", mask, 8) for mask in (6, 2, 4)]


def siblings(own):
    return own + [swap(v, "cells", 1, 8) for v in own]


def gathered_places(i):
    return [i ^ mask for mask in (0, 6, 2, 4, 1, 7, 3, 5)]


def aligned(index, size):
    return pl.ds(pl.multiple_of(index * size, size), size)


def split(x):
    high = x.astype(BF)
    return high, (x - high.astype(F32)).astype(BF)


def halves(x):
    return jnp.concatenate(split(x), 0)


def dot(a, b):
    return jnp.dot(a, b, preferred_element_type=F32)


def dot_nt(a, b):
    return lax.dot_general(a, b, NT, preferred_element_type=F32)


def fold(x):
    n = x.shape[0] // 2
    return x[:n] + x[n:]


def call(kernel, shapes, ints, args, scratch=()):
    n, o = len(args), len(shapes)

    def whole(ints_ref, *refs):
        kernel(ints_ref, refs[:n], refs[n : n + o], refs[n + o :])

    return pl.pallas_call(
        whole,
        out_shape=tuple(jax.ShapeDtypeStruct(s, t) for s, t in shapes),
        in_specs=[pl.BlockSpec(memory_space=pltpu.SMEM)] + [pl.BlockSpec()] * n,
        scratch_shapes=list(scratch),
        compiler_params=PARAMS,
    )(ints, *args)


def after(x, *others):
    return lax.optimization_barrier((x,) + others)[0]


def zones_of(owner_ref):
    rows = owner_ref.shape[1]
    owner = owner_ref[...].astype(F32)
    if rows < LANES:
        owner = jnp.concatenate([owner, jnp.zeros((1, LANES - rows), F32)], 1)
    owner = jnp.transpose(jnp.broadcast_to(owner, (TILE, LANES)))[:rows, 0:1]
    lanes = lax.broadcasted_iota(jnp.int32, (rows, LANES), 1).astype(F32)
    return jnp.where(owner == lanes, 1.0, 0.0)


def news_of(levels, zones, partner_ref):
    rows, total = levels.shape
    ids = lax.broadcasted_iota(jnp.int32, (TILE, total), 0)
    chosen = jnp.where(ids == partner_ref[...], 1.0, 0.0)
    number = jnp.maximum(jnp.sum(chosen, axis=1, keepdims=True), 1.0)
    chosen = chosen.astype(BF)
    high, low = split(levels)
    density = (dot_nt(chosen, high) + dot_nt(chosen, low)) / number
    tile = jnp.concatenate([density, jnp.zeros((TILE, LANES - rows), F32)], 1)
    column = jnp.sum(zones * levels[:, 0:1], axis=0, keepdims=True)
    at = lax.broadcasted_iota(jnp.int32, (TILE, LANES), 0)
    return jnp.where(at == COLUMN_ROW, column, tile)


def message_kernel(ints_ref, args, outs, scratch):
    spectra_ref, section_ref, level_ref, partner_ref, owner_ref = args
    block = spectra_ref.shape[0]
    k = ints_ref[0]
    news = halves(news_of(level_ref[...], zones_of(owner_ref), partner_ref))
    part = outs[0].shape[0] - 2 * TILE - block
    width = outs[0].shape[1]
    if width > LANES:
        news = jnp.concatenate([news, jnp.zeros((2 * TILE, width - LANES), BF)], 1)
    for mask, out in enumerate(outs):
        out[:block, :] = spectra_ref[...]
        out[block : block + part, :] = section_ref[aligned(k ^ mask, part), :]
        out[block + part :, :] = news


def pack_kernel(ints_ref, args, outs, scratch):
    packed_ref, news_ref = outs
    k = ints_ref[0]
    part = packed_ref.shape[0] - 2 * TILE
    total = None
    for mask, ref in enumerate(args):
        below = ref.shape[0] - 2 * TILE
        packed_ref[:part, aligned(k ^ mask, ref.shape[1])] = ref[below - part : below, :]
        news = fold(ref[below:, :LANES].astype(F32))
        news_ref[aligned(k ^ mask, TILE), :] = news
        total = news if total is None else total + news
    packed_ref[part:, :] = jnp.concatenate(
        [halves(total), jnp.zeros((2 * TILE, packed_ref.shape[1] - LANES), BF)], 1
    )


def escape_of(column, zones, block):
    escape = 1.0 / (1.0 + depth_scale * column[COLUMN_ROW : COLUMN_ROW + 1] / block)
    return jnp.sum(zones * escape, axis=1, keepdims=True)


def density_of(news_ref, first, ne, slab):
    parts = []
    for z in range(ne):
        parts.append(jnp.transpose(news_ref[aligned(first + z, TILE), :])[:slab])
    return jnp.concatenate(parts, 0)


def tables_kernel(cells, energies):
    def kernel(ints_ref, args, outs, scratch):
        source_ref, hop_ref, rad_ref = args
        pick_ref, move_ref, drain_ref = outs
        chunks, levels, step = pick_ref.shape
        part = chunks * step // (cells * energies)
        starts = [c * energies * part + z * part for z in range(energies) for c in range(cells)]
        acc = jnp.zeros((levels, levels), F32)
        ids = lax.broadcasted_iota(jnp.int32, (levels, step), 0)
        each = step // part
        for n in range(chunks):

            def row(ref):
                pieces = [ref[0:1, at : at + part] for at in starts[n * each : (n + 1) * each]]
                return pieces[0] if each == 1 else jnp.concatenate(pieces, 1)

            source = row(source_ref)
            target = source + row(hop_ref)
            target = jnp.where(target >= levels, target - levels, target)
            pick = jnp.where(ids == source, 1.0, 0.0)
            move = (jnp.where(ids == target, 1.0, 0.0) - pick).astype(BF)
            pick_ref[n] = pick.astype(BF)
            move_ref[n] = move
            rad = row(rad_ref)
            high = rad.astype(BF).astype(F32)
            acc += dot_nt((pick * high).astype(BF), move)
            acc += dot_nt((pick * (rad - high)).astype(BF), move)
        drain_ref[...] = acc

    return kernel


def scatter(pairs, k, rate_refs, pick_ref, move_ref, groups):
    rows = pairs.shape[0] // (2 * groups)
    step = pick_ref.shape[2]
    acc = jnp.zeros(pairs.shape, F32)
    for mask, ref in enumerate(rate_refs):
        each = ref.shape[1] // step
        for inner in range(each):
            n = (k ^ mask) * each + inner
            rate = ref[:, inner * step : (inner + 1) * step].astype(F32)
            picked = dot(pairs, pick_ref[n])
            parts = []
            for g in range(groups):
                parts.append(halves(rate * fold(picked[2 * g * rows : 2 * (g + 1) * rows])))
            flux = parts[0] if groups == 1 else jnp.concatenate(parts, 0)
            acc += dot_nt(flux, move_ref[n])
    return [fold(acc[2 * g * rows : 2 * (g + 1) * rows]) for g in range(groups)]


def drained(pairs, drain_ref):
    high, low = split(drain_ref[...])
    return fold(dot(pairs, high) + dot(pairs, low))


def first_kernel(block):
    def kernel(ints_ref, args, outs, scratch):
        level_ref, column_ref, owner_ref, partner_ref, pick_ref, move_ref, drain_ref, *rates = args
        levels = level_ref[...]
        zones = zones_of(owner_ref)
        escape = escape_of(column_ref[...], zones, block)
        for _ in range(2):
            pairs = halves(levels)
            (moved,) = scatter(pairs, ints_ref[0], rates, pick_ref, move_ref, 1)
            levels = levels + level_step * (moved + escape * drained(pairs, drain_ref))
        outs[0][...] = levels
        outs[1][...] = news_of(levels, zones, partner_ref)

    return kernel


def second_kernel(ints_ref, args, outs, scratch):
    level_ref, pick_ref, move_ref, drain_ref, *rates = args
    k = ints_ref[0]
    levels = level_ref[...]
    pairs = halves(levels)
    (moved,) = scatter(pairs, k, rates, pick_ref, move_ref, 1)
    u = levels + level_step * moved
    v = level_step * drained(pairs, drain_ref)
    pu, pv = halves(u), halves(v)
    mu, mv = scatter(jnp.concatenate([pu, pv], 0), k, rates, pick_ref, move_ref, 2)
    outs[0][0] = u + level_step * mu
    outs[0][1] = v + level_step * (mv + drained(pu, drain_ref))
    outs[0][2] = level_step * drained(pv, drain_ref)


def final_kernel(block, ne, slab):
    def kernel(ints_ref, args, outs, scratch):
        owner_ref, term_ref, current_ref, product_ref, *tiles = args
        (news_ref,) = scratch
        for mask, ref in enumerate(tiles[:ne]):
            news_ref[aligned(ints_ref[0] ^ mask, TILE), :] = ref[...]
        column = tiles[ne][...]
        for ref in tiles[ne + 1 :]:
            column = column + ref[...]
        escape = escape_of(column, zones_of(owner_ref), block)
        outs[1][...] = term_ref[0] + escape * (term_ref[1] + escape * term_ref[2])
        density = density_of(news_ref, 0, ne, slab)
        summed = density[:, 0:1] * product_ref[0]
        for p in range(1, product_ref.shape[0]):
            summed = summed + density[:, p : p + 1] * product_ref[p]
        outs[0][...] = current_ref[...] + boltz_step * summed

    return kernel


def place(ints_ref, parts, row_ref):
    for mask, ref in enumerate(parts):
        row_ref[:, aligned(ints_ref[0] ^ mask, ref.shape[1])] = ref[: row_ref.shape[0], :]


def product_of(ints_ref, row_ref, parts, p):
    total = None
    for n, ref in enumerate(parts):
        width = ref.shape[2]
        lhs = row_ref[...] if len(parts) == 1 else row_ref[:, aligned(ints_ref[2 + n], width)]
        term = dot_nt(lhs, ref[p])
        total = term if total is None else total + term
    return total


def first_product_kernel(ne, slab):
    def kernel(ints_ref, args, outs, scratch):
        news_ref, *args = args
        spectra, parts, (row_ref,) = args[:ne], args[ne:], scratch
        place(ints_ref, spectra, row_ref)
        density = density_of(news_ref, 0, ne, slab)
        summed = None
        for p in range(parts[0].shape[0]):
            term = density[:, p : p + 1] * product_of(ints_ref, row_ref, parts, p)
            summed = term if summed is None else summed + term
        current = spectra[0][: row_ref.shape[0], :].astype(F32) + boltz_step * summed
        outs[0][...] = current
        outs[1][...] = current.astype(BF)

    return kernel


def second_product_kernel(ne):
    def kernel(ints_ref, args, outs, scratch):
        place(ints_ref, args[:ne], scratch[0])
        for p in range(outs[0].shape[0]):
            outs[0][p] = product_of(ints_ref, scratch[0], args[ne:], p)

    return kernel


def rates_kernel(ne, small):
    def kernel(ints_ref, args, outs, scratch):
        spectra, parts, (row_ref, rate_ref) = args[:ne], args[ne:], scratch
        outs, column_ref = outs[:ne], outs[ne]
        place(ints_ref, spectra, row_ref)
        row = row_ref[...]
        column = None
        for n, ref in enumerate(parts):
            part = ref.shape[0] - 2 * TILE
            rates = jax.nn.softplus(dot_nt(row, ref[:part, :])).astype(BF)
            if small:
                rate_ref[:, aligned(ints_ref[2 + n], part)] = rates
            else:
                rate_ref[:, n * part : (n + 1) * part] = rates
            own = fold(ref[part:, :LANES].astype(F32))
            column = own if column is None else column + own
        column_ref[...] = column
        for mask, out in enumerate(outs):
            out[...] = rate_ref[aligned(ints_ref[0] ^ mask, out.shape[0]), :]

    return kernel


def body(
    distribution,
    operators,
    sections,
    populations,
    cell_owner,
    partner_of,
    source,
    level_hop,
    radiative,
):
    nc = lax.axis_size("cells")
    ne = lax.axis_size("energy")
    i = lax.axis_index("cells")
    k = lax.axis_index("energy")
    slab, level_total = populations.shape
    block, width = distribution.shape
    partner_total, outs, _ = operators.shape
    reactions = source.shape[0]
    part = sections.shape[0] // ne
    small = nc == 8
    places = gathered_places(i) if small else []
    ints = jnp.stack([v.astype(jnp.int32) for v in [k, i] + places])
    partner_row = partner_of.reshape(1, level_total)
    owner_row = cell_owner.reshape(1, slab)

    messages = call(
        message_kernel,
        [((block + part + 2 * TILE, width), BF)] * ne,
        ints,
        [distribution, sections, populations, partner_row, owner_row],
    )
    got = {m: swap(messages[m], "energy", m, ne) for m in range(ne - 1, 0, -1)}
    spectra = [messages[0]] + [got[m] for m in range(1, ne)]
    packed_shape = [((part + 2 * TILE, ne * width), BF), ((ne * TILE, LANES), F32)]
    packed_args = list(spectra)
    if small:
        operator_parts = chips(operators)
        packed_args[1] = after(packed_args[1], *operator_parts[1:])
        packed, density = call(pack_kernel, packed_shape, ints, packed_args)
        operator_parts = siblings(operator_parts)
        section_parts = chips(packed)
    else:
        packed, density = call(pack_kernel, packed_shape, ints, packed_args)
        operator_parts = [lax.all_gather(operators, "cells", axis=2, tiled=True)]
        every = lax.all_gather(packed, "cells")
        section_parts = [every[n] for n in range(nc)]

    chunks = ((max(1, reactions // 512), level_total, min(512, reactions)), BF)
    pick, move, drain = call(
        tables_kernel(nc, ne),
        [chunks, chunks, ((level_total, level_total), F32)],
        ints,
        [v.reshape(1, reactions) for v in (source, level_hop, radiative)],
    )

    row = pltpu.VMEM((block, ne * width), BF)

    current, later = call(
        first_product_kernel(ne, slab),
        [((block, outs), F32), ((block, outs), BF)],
        ints,
        [density] + spectra + operator_parts,
        [row],
    )
    later = others(later, ne)
    if small:
        section_parts = siblings(section_parts[:1] + [after(v, later[1], later[2]) for v in section_parts[1:]])

    def rates_of(spectra):
        *rates, column = call(
            rates_kernel(ne, small),
            [((slab, nc * part), BF)] * ne + [((TILE, LANES), F32)],
            ints,
            list(spectra) + section_parts,
            [row, pltpu.VMEM((block, nc * part), BF)],
        )
        got = {m: swap(rates[m], "energy", m, ne) for m in range(ne - 1, 0, -1)}
        return [rates[0]] + [got[m] for m in range(1, ne)], column

    rates, column = rates_of(spectra)
    (products,) = call(
        second_product_kernel(ne),
        [((partner_total, block, outs), F32)],
        ints,
        later + operator_parts,
        [row],
    )
    later_rates, _ = rates_of(later)
    rates[0] = after(rates[0], later_rates[0], products)
    levels, news = call(
        first_kernel(block),
        [(populations.shape, F32), ((TILE, LANES), F32)],
        ints,
        [populations, column, owner_row, partner_row, pick, move, drain] + rates,
    )
    if small:
        news = after(news, later_rates[1], later_rates[3])
    news = others(news, ne)
    column = sum(news[1:], news[0])
    if small:
        column = column + swap(column, "cells", 1, nc)
    columns = chips(column) if small else [lax.psum(column, "cells")]
    (terms,) = call(
        second_kernel,
        [((3,) + populations.shape, F32)],
        ints,
        [levels, pick, move, drain] + later_rates,
    )
    return call(
        final_kernel(block, ne, slab),
        [((block, outs), F32), (populations.shape, F32)],
        ints,
        [owner_row, terms, current, products] + news + columns,
        [pltpu.VMEM((ne * TILE, LANES), F32)],
    )


def solution(mesh):
    return jax.shard_map(
        body,
        mesh=mesh,
        in_specs=(
            P("cells", "energy"),
            P(None, "energy", "cells"),
            P("cells", "energy"),
            P(("cells", "energy"), None),
            P(("cells", "energy"), None),
            P(),
            P(),
            P(),
            P(),
        ),
        out_specs=(P("cells", "energy"), P(("cells", "energy"), None)),
        check_vma=False,
    )
```
